512 devices in a mesh: aux: 64 (over y, z), occ: 8 (over x, core).
Axes of the slice: x: 4, y: 4, z: 16, core: 2. Of those that a mesh axis runs over, the one named last changes fastest.
Arguments:
- factor_tiles: bfloat16 [128, 24, 4, 128, 128], P('aux'), may hold values from -1 to 1
- tile_cols: int32 [128, 24, 4], P('aux'), may hold values from 0 to 23, as said below
- coeffs: bfloat16 [3072, 256], P(None, 'occ'), may hold values from -0.25 to 0.25
- pair_owner: int32 [576], P('aux'), may hold values from 0 to 575, each once
Outputs:
- exchange_tiles: float32 [576, 128, 128], P('aux', 'occ')
The draws below stay inside these ranges and needn't reach their ends.
Inputs may be any that keep to these rules, and one draw needn't show every extreme that they name: `tile_cols`: for each auxiliary function and basis block row, the 4 listed column blocks are distinct. `pair_owner`: each basis block pair appears exactly once.
All inputs are finite; a program needn't handle non-finite values.
Results may differ from the reference program's by a relative error of at most 0.0015.
Values may be sent and summed in bfloat16 or wider, within the bound.
A program may use at most 128 MiB of HBM per device.

```python
import jax
import jax.numpy as jnp
from jax import lax

BLK = 128
NB = 24
BASIS = 3072
OCC = 256
S = 4
QD = 2
AUXF = 128
N_AUX = 64


def draw_tile_cols(key, part):
    scores = jax.random.randint(key, (AUXF, NB, NB), 0, 1 << 20) * NB + jnp.arange(NB, dtype=jnp.int32)
    ordering = jnp.argsort(scores, axis=-1, stable=True)
    return ordering[..., :S].astype(jnp.int32)


def block_scale(key, shape, cuts, low, top_value):
    def one(dim, parts):
        draws = jax.random.uniform(jax.random.fold_in(jax.random.fold_in(key, 6), dim), (parts,), jnp.float32, low / len(cuts), top_value / len(cuts))
        return jnp.repeat(jnp.exp(draws), shape[dim] // parts).reshape((-1,) + (1,) * (len(shape) - dim - 1))

    gain = one(*cuts[0])
    for cut in cuts[1:]:
        gain = gain * one(*cut)
    return gain


def centred(own_key, dims, width, most, pieces=(), held_as=jnp.bfloat16):
    drawn = jax.random.normal(own_key, dims, jnp.float32) * width
    if len(pieces) > 0:
        drawn = block_scale(own_key, dims, pieces, -0.22, 0.18) * drawn
    return jnp.clip(drawn, min=-most, max=most).astype(held_as)


def setup_inputs(seed: int = 0) -> dict:
    arg_keys = jax.random.split(jax.random.key(seed), 5)
    return {
        "factor_tiles": centred(arg_keys[0], (AUXF, NB, S, BLK, BLK), ((QD * N_AUX * OCC) ** -0.25), 1.0, ((0, 64),)),
        "tile_cols": draw_tile_cols(jax.random.fold_in(arg_keys[4], 71), 0),
        "coeffs": centred(arg_keys[2], (BASIS, OCC), (S * BLK) ** -0.5, 0.25, ((1, 8),)),
        "pair_owner": jax.random.permutation(arg_keys[3], NB * NB).astype(jnp.int32),
    }


def reference(factor_tiles, tile_cols, coeffs, pair_owner):
    blocks = coeffs.reshape(NB, BLK, OCC)

    def transform(inputs):
        slab_tiles, slab_cols = inputs
        picked = blocks[slab_cols]
        product = jnp.einsum('msrl,msli->mri', slab_tiles.astype(jnp.float32), picked.astype(jnp.float32))
        return product.astype(jnp.bfloat16)

    halves = lax.map(transform, (factor_tiles, tile_cols))
    stacked = jnp.transpose(halves, (1, 2, 0, 3)).reshape(NB, BLK, AUXF * OCC)

    def one_tile(pair_index):
        row_part = stacked[pair_index // NB]
        col_part = stacked[pair_index % NB]
        return jnp.dot(row_part, col_part.T, preferred_element_type=jnp.float32)

    return lax.map(one_tile, pair_owner)
```

```python
import jax
import jax.numpy as jnp
from jax import lax
from jax.experimental import pallas as pl
from jax.experimental.pallas import tpu as pltpu
from jax.sharding import PartitionSpec as P

NT = (((1,), (1,)), ((), ()))


def partial_kernel(cols, owners, share, factor, coeffs_t, out, half, mine, tiles):
    m = pl.program_id(0)
    aux_count, _, entries, blk, _ = factor.shape
    occ = coeffs_t.shape[0]
    nb = cols.shape[0] // (aux_count * entries)
    rows = out.shape[1]
    for q in range(aux_count):
        left, right = [], []
        for s in range(entries):
            col = cols[(q * nb + m) * entries + s]
            left.append(factor[q, 0, s])
            right.append(coeffs_t[:, pl.ds(pl.multiple_of(col * blk, blk), blk)])
        done = lax.dot_general(
            jnp.concatenate(left, axis=1),
            jnp.concatenate(right, axis=1),
            NT,
            preferred_element_type=jnp.float32,
        )
        half[pl.ds(pl.multiple_of(m * blk, blk), blk), q * occ : (q + 1) * occ] = done.astype(
            jnp.bfloat16
        )
    first = pl.multiple_of(m * blk + share[0] * rows, rows)
    mine[pl.ds(pl.multiple_of(m * rows, rows), rows), :] = half[pl.ds(first, rows), :]

    @pl.when(m == nb - 1)
    def _():
        def pair(p, carry):
            part = half[pl.ds(pl.multiple_of(p * 2 * blk, 2 * blk), 2 * blk), :]
            prod = lax.dot_general(mine[...], part, NT, preferred_element_type=jnp.float32)
            tiles[2 * p] = prod[:, :blk]
            tiles[2 * p + 1] = prod[:, blk:]
            return carry

        lax.fori_loop(0, nb // 2, pair, 0)

        def pick(k, carry):
            pair_index = owners[k]
            a, b = pair_index // nb, pair_index % nb
            out[k] = tiles[b, pl.ds(pl.multiple_of(a * rows, rows), rows), :]
            return carry

        lax.fori_loop(0, nb * nb, pick, 0)


def shards(factor_tiles, tile_cols, coeffs, pair_owner):
    aux_count, nb, entries, blk, _ = factor_tiles.shape
    occ_ways = lax.axis_size("occ")
    rows = blk // occ_ways
    occ = coeffs.shape[1] * occ_ways
    coeffs_t = lax.all_gather(coeffs.T, "occ", axis=0, tiled=True)
    owners = lax.all_gather(pair_owner, "aux", axis=0, tiled=True)
    share = lax.axis_index("occ").astype(jnp.int32).reshape(1)
    partial = pl.pallas_call(
        partial_kernel,
        grid_spec=pltpu.PrefetchScalarGridSpec(
            num_scalar_prefetch=3,
            grid=(nb,),
            in_specs=[
                pl.BlockSpec((aux_count, 1, entries, blk, blk), lambda m, *_: (0, m, 0, 0, 0)),
                pl.BlockSpec((occ, nb * blk), lambda m, *_: (0, 0)),
            ],
            out_specs=pl.BlockSpec((nb * nb, rows, blk), lambda m, *_: (0, 0, 0)),
            scratch_shapes=[
                pltpu.VMEM((nb * blk, aux_count * occ), jnp.bfloat16),
                pltpu.VMEM((nb * rows, aux_count * occ), jnp.bfloat16),
                pltpu.VMEM((nb, nb * rows, blk), jnp.float32),
            ],
        ),
        out_shape=jax.ShapeDtypeStruct((nb * nb, rows, blk), jnp.float32),
        compiler_params=pltpu.CompilerParams(vmem_limit_bytes=48 * 2**20),
    )(tile_cols.reshape(-1), owners, share, factor_tiles, coeffs_t)
    return lax.psum_scatter(partial, "aux", scatter_dimension=0, tiled=True)


def solution(mesh):
    placed = (P("aux", None, None, None, None), P("aux", None, None), P(None, "occ"), P("aux"))
    return jax.shard_map(
        shards, mesh=mesh, in_specs=placed, out_specs=P("aux", "occ", None), check_vma=False
    )
```

```python
import jax
import jax.numpy as jnp
from jax import lax
from jax.experimental import pallas as pl
from jax.experimental.pallas import tpu as pltpu
from jax.sharding import PartitionSpec as P

NT = (((1,), (1,)), ((), ()))
NY, NZ = 4, 16
MESH = pl.DeviceIdType.MESH
GROUPS = [[8]] + [[k, NZ - k] for k in range(7, 0, -1)] + [[0]]
AHEAD, LAG = 2, 1


def partial_kernel(cols, share, factor, coeffs_t, tiles, half, mine):
    m = pl.program_id(0)
    aux_count, _, entries, blk, _ = factor.shape
    occ = coeffs_t.shape[0]
    nb = cols.shape[0] // (aux_count * entries)
    rows = tiles.shape[1] // nb
    for q in range(aux_count):
        left, right = [], []
        for s in range(entries):
            col = cols[(q * nb + m) * entries + s]
            left.append(factor[q, 0, s])
            right.append(coeffs_t[:, pl.ds(pl.multiple_of(col * blk, blk), blk)])
        done = lax.dot_general(
            jnp.concatenate(left, axis=1),
            jnp.concatenate(right, axis=1),
            NT,
            preferred_element_type=jnp.float32,
        )
        half[pl.ds(pl.multiple_of(m * blk, blk), blk), q * occ : (q + 1) * occ] = done.astype(
            jnp.bfloat16
        )
    first = pl.multiple_of(m * blk + share[0] * rows, rows)
    mine[pl.ds(pl.multiple_of(m * rows, rows), rows), :] = half[pl.ds(first, rows), :]

    @pl.when(m == nb - 1)
    def _():
        def pair(p, carry):
            part = half[pl.ds(pl.multiple_of(p * 2 * blk, 2 * blk), 2 * blk), :]
            prod = lax.dot_general(mine[...], part, NT, preferred_element_type=jnp.float32)
            tiles[2 * p] = prod[:, :blk]
            tiles[2 * p + 1] = prod[:, blk:]
            return carry

        lax.fori_loop(0, nb // 2, pair, 0)


def scatter_kernel(places, tiles, out, s_a, r_a, s_b, r_b, s_z, r_z, a_out, a_in, b_out, b_in, z_out, z_in):
    me = lax.axis_index("aux")
    y, z = me // NZ, me % NZ
    own, rows = out.shape[0], out.shape[1]
    size = own * rows
    cut = (own + 1) // 2 * rows
    y_to = [(y + 1) % NY * NZ + z, (y + NY - 1) % NY * NZ + z]
    z_to = [y * NZ + (z + 1) % NZ, y * NZ + (z + NZ - 1) % NZ]

    barrier = pltpu.get_barrier_semaphore()
    for other in y_to + z_to:
        pl.semaphore_signal(barrier, inc=1, device_id={"aux": other}, device_id_type=MESH)
    pl.semaphore_wait(barrier, 4)

    def chunk(up, d):
        first = ((y + up) % NY * NZ + (z + d) % NZ) * own
        picked = [
            tiles[places[first + t]] for t in range(own)
        ]
        return jnp.concatenate(picked, axis=0)

    def send(src, dst, out_sem, in_sem, other):
        return pltpu.make_async_remote_copy(
            src_ref=src, dst_ref=dst, send_sem=out_sem, recv_sem=in_sem,
            device_id={"aux": other}, device_id_type=MESH,
        )

    def way(d):
        return 0 if 1 <= d <= NZ // 2 else 1

    def copy_a(d):
        return send(s_a.at[d], r_a.at[d], a_out.at[d], a_in.at[d], y_to[way(d)])

    def copy_b(w, d):
        return send(s_b.at[w, d], r_b.at[w, d], b_out.at[w, d], b_in.at[w, d], y_to[w])

    def copy_z(w, s):
        if s == 0:
            piece = pl.ds(0, cut) if w == 0 else pl.ds(cut, size - cut)
            return send(s_z.at[w, 0, piece], r_z.at[w, 0, piece], z_out.at[w, 0], z_in.at[w, 0], z_to[w])
        return send(s_z.at[w, s], r_z.at[w, s], z_out.at[w, s], z_in.at[w, s], z_to[w])

    def first_hop(d):
        s_a[d] = chunk(2, d)
        copy_a(d).start()

    def second_hop(d):
        for w, up in ((0, 1), (1, NY - 1)):
            part = chunk(up, d)
            if way(d) == w:
                copy_a(d).wait_recv()
                part = part + r_a[d]
            s_b[w, d] = part
            copy_b(w, d).start()

    def column(d):
        copy_b(0, d).wait_recv()
        copy_b(1, d).wait_recv()
        return chunk(0, d) + r_b[0, d] + r_b[1, d]

    def chain(s):
        if s == 0:
            part = column(NZ // 2)
            s_z[0, 0, :cut] = part[:cut]
            s_z[1, 0, cut:] = part[cut:]
            copy_z(0, 0).start()
            copy_z(1, 0).start()
            return
        if s == NZ // 2:
            part = column(0)
            for w in range(2):
                copy_z(w, s - 1).wait_recv()
            part = part + r_z[0, s - 1] + r_z[1, s - 1]
            for t in range(own):
                out[t] = part[t * rows : (t + 1) * rows]
            return
        for w, d in ((0, NZ // 2 - s), (1, NZ // 2 + s)):
            part = column(d)
            copy_z(w, s - 1).wait_recv()
            if s == 1:
                piece = slice(0, cut) if w == 0 else slice(cut, size)
                came = part[piece] + r_z[w, 0, piece]
                part = jnp.concatenate([came, part[cut:]] if w == 0 else [part[:cut], came], axis=0)
            else:
                part = part + r_z[w, s - 1]
            s_z[w, s] = part
            copy_z(w, s).start()

    count = len(GROUPS)
    for i in range(-AHEAD, count + LAG):
        if i + AHEAD < count:
            for d in GROUPS[i + AHEAD]:
                first_hop(d)
        if 0 <= i < count:
            for d in GROUPS[i]:
                second_hop(d)
        if i - LAG >= 0:
            chain(i - LAG)
    for d in range(NZ):
        copy_a(d).wait_send()
        for w in range(2):
            copy_b(w, d).wait_send()
    for s in range(NZ // 2):
        for w in range(2):
            copy_z(w, s).wait_send()


def shards(factor_tiles, tile_cols, coeffs, pair_owner):
    aux_count, nb, entries, blk, _ = factor_tiles.shape
    occ_ways = lax.axis_size("occ")
    rows = blk // occ_ways
    occ = coeffs.shape[1] * occ_ways
    own = pair_owner.shape[0]
    coeffs_t = lax.all_gather(coeffs.T, "occ", axis=0, tiled=True)
    place = (pair_owner % nb) * nb + pair_owner // nb
    places = lax.all_gather(place, "aux", axis=0, tiled=True)
    share = lax.axis_index("occ").astype(jnp.int32).reshape(1)
    tiles = pl.pallas_call(
        partial_kernel,
        grid_spec=pltpu.PrefetchScalarGridSpec(
            num_scalar_prefetch=2,
            grid=(nb,),
            in_specs=[
                pl.BlockSpec((aux_count, 1, entries, blk, blk), lambda m, *_: (0, m, 0, 0, 0)),
                pl.BlockSpec((occ, nb * blk), lambda m, *_: (0, 0)),
            ],
            out_specs=pl.BlockSpec((nb, nb * rows, blk), lambda m, *_: (0, 0, 0)),
            scratch_shapes=[
                pltpu.VMEM((nb * blk, aux_count * occ), jnp.bfloat16),
                pltpu.VMEM((nb * rows, aux_count * occ), jnp.bfloat16),
            ],
        ),
        out_shape=jax.ShapeDtypeStruct((nb, nb * rows, blk), jnp.float32),
        compiler_params=pltpu.CompilerParams(vmem_limit_bytes=48 * 2**20),
    )(tile_cols.reshape(-1), share, factor_tiles, coeffs_t)
    piece = (own * rows, blk)
    dma = pltpu.SemaphoreType.DMA
    return pl.pallas_call(
        scatter_kernel,
        in_specs=[pl.BlockSpec(memory_space=pltpu.SMEM), pl.BlockSpec(memory_space=pltpu.VMEM)],
        out_specs=pl.BlockSpec(memory_space=pltpu.VMEM),
        out_shape=jax.ShapeDtypeStruct((own, rows, blk), jnp.float32),
        scratch_shapes=[
            pltpu.VMEM((NZ, *piece), jnp.float32),
            pltpu.VMEM((NZ, *piece), jnp.float32),
            pltpu.VMEM((2, NZ, *piece), jnp.float32),
            pltpu.VMEM((2, NZ, *piece), jnp.float32),
            pltpu.VMEM((2, NZ // 2, *piece), jnp.float32),
            pltpu.VMEM((2, NZ // 2, *piece), jnp.float32),
            dma((NZ,)), dma((NZ,)),
            dma((2, NZ)), dma((2, NZ)),
            dma((2, NZ // 2)), dma((2, NZ // 2)),
        ],
        compiler_params=pltpu.CompilerParams(
            collective_id=0, has_side_effects=True, vmem_limit_bytes=48 * 2**20
        ),
    )(places, tiles.reshape(nb * nb, rows, blk))


def solution(mesh):
    placed = (P("aux", None, None, None, None), P("aux", None, None), P(None, "occ"), P("aux"))
    return jax.shard_map(
        shards, mesh=mesh, in_specs=placed, out_specs=P("aux", "occ", None), check_vma=False
    )
```

```python
import jax
import jax.numpy as jnp
from jax import lax
from jax.experimental import pallas as pl
from jax.experimental.pallas import tpu as pltpu
from jax.sharding import PartitionSpec as P

NT = (((1,), (1,)), ((), ()))
NX, NY, NZ = 4, 4, 16
MESH = pl.DeviceIdType.MESH
GROUPS = [[8]] + [[k, NZ - k] for k in range(7, 0, -1)] + [[0]]
AHEAD, LAG = 2, 1
STAGES = 4


def kernel(
    cols, owner, factor, coeffs_t, out,
    f_buf, c_all, half, mine, tiles, by_y, by_z, place,
    s_a, r_a, s_b, r_b, s_z, r_z,
    f_in, g_out, g_in, py_out, py_in, pz_out, pz_in, p_in,
    a_out, a_in, b_out, b_in, z_out, z_in,
):
    me, occ = lax.axis_index("aux"), lax.axis_index("occ")
    y, z = me // NZ, me % NZ
    x, core = occ // 2, occ % 2
    aux_count, nb, entries, blk, _ = f_buf.shape
    own, rows = out.shape[0], out.shape[1]
    share = coeffs_t.shape[0]
    all_occ = c_all.shape[1]
    size = own * rows
    cut = (own + 1) // 2 * rows
    step = nb // STAGES

    def up_y(k):
        return (y + k) % NY * NZ + z

    def up_z(k):
        return y * NZ + (z + k) % NZ

    def peer(dx, other_core=False):
        return (x + dx) % NX * 2 + (1 - core if other_core else core)

    loads = [
        pltpu.make_async_copy(
            factor.at[:, pl.ds(n * step, step)], f_buf.at[:, pl.ds(n * step, step)], f_in.at[n]
        )
        for n in range(STAGES)
    ]
    for load in loads:
        load.start()

    barrier = pltpu.get_barrier_semaphore()
    aux_peers = [up_y(k) for k in range(1, NY)] + [up_z(k) for k in range(1, NZ)]
    occ_peers = [peer(1), peer(NX - 1), peer(0, True)]
    for other in aux_peers:
        pl.semaphore_signal(barrier, inc=1, device_id={"aux": other}, device_id_type=MESH)
    for other in occ_peers:
        pl.semaphore_signal(barrier, inc=1, device_id={"occ": other}, device_id_type=MESH)

    for b in range(nb):
        c_all[b, pl.ds(pl.multiple_of(occ * share, share), share), :] = coeffs_t[
            :, b * blk : (b + 1) * blk
        ]
    lane = lax.broadcasted_iota(jnp.int32, (1, 128), 1)
    codes = jnp.zeros((1, 128), jnp.int32)
    for t in range(own):
        pair_index = owner[t]
        codes = jnp.where(lane == t, (pair_index % nb) * nb + pair_index // nb, codes)
    by_y[y] = codes
    pl.semaphore_wait(barrier, len(aux_peers) + len(occ_peers))

    def send(src, dst, out_sem, in_sem, **other):
        return pltpu.make_async_remote_copy(
            src_ref=src, dst_ref=dst, send_sem=out_sem, recv_sem=in_sem,
            device_id=other, device_id_type=MESH,
        )

    def block(who, part):
        lo, count = (0, nb) if part is None else (part * (nb // 2), nb // 2)
        return c_all.at[pl.ds(lo, count), pl.ds(pl.multiple_of(who * share, share), share)]

    def pass_on(n, who, part, to):
        ref = block(who, part)
        return send(ref, ref, g_out.at[n], g_in.at[n], occ=to)

    right, left, mate = peer(1), peer(NX - 1), peer(0, True)
    moves = [
        (occ, peer(-1 + NX), 0, right),
        (occ, peer(1), 1, left),
        (occ, peer(-1 + NX), 1, right),
        (occ, peer(1), 0, left),
        (peer(-1 + NX), peer(2), 0, right),
        (peer(1), peer(2), 1, left),
        (occ, mate, None, mate),
        (peer(-1 + NX), peer(-1 + NX, True), 0, mate),
        (peer(1), peer(1, True), 1, mate),
        (peer(-1 + NX), peer(-1 + NX, True), 1, mate),
        (peer(1), peer(1, True), 0, mate),
        (peer(2), peer(2, True), 0, mate),
        (peer(2), peer(2, True), 1, mate),
    ]

    def go(n):
        pass_on(n, moves[n][0], moves[n][2], moves[n][3]).start()

    def got(n):
        pass_on(n, moves[n][1], moves[n][2], moves[n][3]).wait_recv()

    def place_y(k, row):
        return send(by_y.at[row], by_y.at[row], py_out.at[k - 1], py_in.at[k - 1], aux=up_y(k))

    def place_z(k, row):
        return send(by_z.at[row], by_z.at[row], pz_out.at[k - 1], pz_in.at[k - 1], aux=up_z(k))

    for n in (0, 1, 2, 3, 6):
        go(n)
    for k in range(1, NY):
        place_y(k, y).start()
    for n, then in ((0, (4, 7)), (1, (5, 8)), (2, (9,)), (3, (10,))):
        got(n)
        for nxt in then:
            go(nxt)
    for k in range(1, NY):
        place_y(k, (y + NY - k) % NY).wait_recv()
    by_z[z] = by_y[...]
    for k in range(1, NZ):
        place_z(k, z).start()
    for n, nxt in ((4, 11), (5, 12)):
        got(n)
        go(nxt)
    for n in range(6, 13):
        got(n)

    for n in range(STAGES):
        loads[n].wait()

        def one(m, carry):
            for q in range(aux_count):
                lhs = jnp.concatenate([f_buf[q, m, s] for s in range(entries)], axis=1)
                rhs = jnp.concatenate([c_all[cols[q, s, m]] for s in range(entries)], axis=1)
                done = lax.dot_general(lhs, rhs, NT, preferred_element_type=jnp.float32)
                half[m, :, q * all_occ : (q + 1) * all_occ] = done.astype(jnp.bfloat16)
            mine[m] = half[m, pl.ds(pl.multiple_of(occ * rows, rows), rows), :]
            return carry

        lax.fori_loop(n * step, (n + 1) * step, one, 0, unroll=2)

    def pair(p, carry):
        lhs = mine[...].reshape(nb * rows, aux_count * all_occ)
        rhs = half[pl.ds(2 * p, 2)].reshape(2 * blk, aux_count * all_occ)
        prod = lax.dot_general(lhs, rhs, NT, preferred_element_type=jnp.float32)
        tiles[pl.ds(2 * p * nb, nb)] = prod[:, :blk].reshape(nb, rows, blk)
        tiles[pl.ds((2 * p + 1) * nb, nb)] = prod[:, blk:].reshape(nb, rows, blk)
        return carry

    lax.fori_loop(0, nb // 2, pair, 0, unroll=2)

    for k in range(1, NZ):
        place_z(k, (z + NZ - k) % NZ).wait_recv()
    fetch = pltpu.make_async_copy(by_z, place, p_in.at[0])
    fetch.start()
    fetch.wait()

    def chunk(up, d):
        yy, zz = (y + up) % NY, (z + d) % NZ
        return jnp.concatenate([tiles[place[zz, yy, 0, t]] for t in range(own)], axis=0)

    def encode(part):
        lead = part.reshape(part.shape[0] // 8, 8, blk)
        top = jnp.max(jnp.abs(lead), axis=0)
        power = jnp.ceil(jnp.log2(jnp.maximum(top, 1e-33)))
        scaled = jnp.round(lead * jnp.exp2(15.0 - power)[None])
        fixed = jnp.clip(scaled, -32767.0, 32767.0).astype(jnp.int32).reshape(part.shape)
        tail = power.astype(jnp.int32)
        return jnp.concatenate([fixed, tail, tail], axis=0).astype(jnp.int16)

    def decode(got_piece):
        wide = got_piece.astype(jnp.int32).astype(jnp.float32)
        n = got_piece.shape[0] - 16
        lead = wide[:n].reshape(n // 8, 8, blk)
        return (lead * jnp.exp2(wide[n : n + 8] - 15.0)[None]).reshape(n, blk)

    def way(d):
        return 0 if 1 <= d <= NZ // 2 else 1

    y_to = [up_y(1), up_y(NY - 1)]
    z_to = [up_z(1), up_z(NZ - 1)]

    def copy_a(d):
        return send(s_a.at[d], r_a.at[d], a_out.at[d], a_in.at[d], aux=y_to[way(d)])

    def copy_b(w, d):
        return send(s_b.at[w, d], r_b.at[w, d], b_out.at[w, d], b_in.at[w, d], aux=y_to[w])

    ends = [cut + 16, size - cut + 16]

    def copy_z(w, s):
        piece = pl.ds(0, ends[w] if s == 0 else size + 16)
        return send(s_z.at[w, s, piece], r_z.at[w, s, piece], z_out.at[w, s], z_in.at[w, s], aux=z_to[w])

    def first_hop(d):
        s_a[d] = encode(chunk(2, d))
        copy_a(d).start()

    def second_hop(d):
        for w, up in ((0, 1), (1, NY - 1)):
            part = chunk(up, d)
            if way(d) == w:
                copy_a(d).wait_recv()
                part = part + decode(r_a[d])
            s_b[w, d] = encode(part)
            copy_b(w, d).start()

    def column(d):
        copy_b(0, d).wait_recv()
        copy_b(1, d).wait_recv()
        return chunk(0, d) + decode(r_b[0, d]) + decode(r_b[1, d])

    def chain(s):
        if s == 0:
            part = column(NZ // 2)
            s_z[0, 0, : ends[0]] = encode(part[:cut])
            s_z[1, 0, : ends[1]] = encode(part[cut:])
            copy_z(0, 0).start()
            copy_z(1, 0).start()
            return
        if s == NZ // 2:
            part = column(0)
            for w in range(2):
                copy_z(w, s - 1).wait_recv()
            part = part + decode(r_z[0, s - 1]) + decode(r_z[1, s - 1])
            out[...] = part.reshape(own, rows, blk)
            return
        for w, d in ((0, NZ // 2 - s), (1, NZ // 2 + s)):
            part = column(d)
            copy_z(w, s - 1).wait_recv()
            if s == 1:
                came = decode(r_z[w, 0, : ends[w]])
                if w == 0:
                    part = jnp.concatenate([part[:cut] + came, part[cut:]], axis=0)
                else:
                    part = jnp.concatenate([part[:cut], part[cut:] + came], axis=0)
            else:
                part = part + decode(r_z[w, s - 1])
            s_z[w, s] = encode(part)
            copy_z(w, s).start()

    count = len(GROUPS)
    for i in range(-AHEAD, count + LAG):
        if i + AHEAD < count:
            for d in GROUPS[i + AHEAD]:
                first_hop(d)
        if 0 <= i < count:
            for d in GROUPS[i]:
                second_hop(d)
        if i - LAG >= 0:
            chain(i - LAG)

    for n in range(13):
        pass_on(n, moves[n][0], moves[n][2], moves[n][3]).wait_send()
    for k in range(1, NY):
        place_y(k, y).wait_send()
    for k in range(1, NZ):
        place_z(k, z).wait_send()
    for d in range(NZ):
        copy_a(d).wait_send()
        for w in range(2):
            copy_b(w, d).wait_send()
    for s in range(NZ // 2):
        for w in range(2):
            copy_z(w, s).wait_send()


def shards(factor_tiles, tile_cols, coeffs, pair_owner):
    aux_count, nb, entries, blk, _ = factor_tiles.shape
    occ_ways = lax.axis_size("occ")
    rows = blk // occ_ways
    occ = coeffs.shape[1] * occ_ways
    own = pair_owner.shape[0]
    piece = (own * rows + 16, blk)
    dma = pltpu.SemaphoreType.DMA
    smem = pl.BlockSpec(memory_space=pltpu.SMEM)
    vmem = pl.BlockSpec(memory_space=pltpu.VMEM)
    return pl.pallas_call(
        kernel,
        in_specs=[smem, smem, pl.BlockSpec(memory_space=pl.ANY), vmem],
        out_specs=vmem,
        out_shape=jax.ShapeDtypeStruct((own, rows, blk), jnp.float32),
        scratch_shapes=[
            pltpu.VMEM(factor_tiles.shape, jnp.bfloat16),
            pltpu.VMEM((nb, occ, blk), jnp.bfloat16),
            pltpu.VMEM((nb, blk, aux_count * occ), jnp.bfloat16),
            pltpu.VMEM((nb, rows, aux_count * occ), jnp.bfloat16),
            pltpu.VMEM((nb * nb, rows, blk), jnp.float32),
            pltpu.VMEM((NY, 1, 128), jnp.int32),
            pltpu.VMEM((NZ, NY, 1, 128), jnp.int32),
            pltpu.SMEM((NZ, NY, 1, 128), jnp.int32),
            pltpu.VMEM((NZ, *piece), jnp.int16),
            pltpu.VMEM((NZ, *piece), jnp.int16),
            pltpu.VMEM((2, NZ, *piece), jnp.int16),
            pltpu.VMEM((2, NZ, *piece), jnp.int16),
            pltpu.VMEM((2, NZ // 2, *piece), jnp.int16),
            pltpu.VMEM((2, NZ // 2, *piece), jnp.int16),
            dma((STAGES,)),
            dma((13,)), dma((13,)),
            dma((NY - 1,)), dma((NY - 1,)),
            dma((NZ - 1,)), dma((NZ - 1,)),
            dma((1,)),
            dma((NZ,)), dma((NZ,)),
            dma((2, NZ)), dma((2, NZ)),
            dma((2, NZ // 2)), dma((2, NZ // 2)),
        ],
        compiler_params=pltpu.CompilerParams(
            collective_id=0, has_side_effects=True, vmem_limit_bytes=48 * 2**20
        ),
    )(jnp.transpose(tile_cols, (0, 2, 1)), pair_owner, factor_tiles, coeffs.T)


def solution(mesh):
    placed = (P("aux", None, None, None, None), P("aux", None, None), P(None, "occ"), P("aux"))
    return jax.shard_map(
        shards, mesh=mesh, in_specs=placed, out_specs=P("aux", "occ", None), check_vma=False
    )
```

```python
import jax
import jax.numpy as jnp
from jax import lax
from jax.experimental import pallas as pl
from jax.experimental.pallas import tpu as pltpu
from jax.sharding import PartitionSpec as P

NT = (((1,), (1,)), ((), ()))
NX, NY, NZ = 4, 4, 16
MESH = pl.DeviceIdType.MESH
ORDER = [8, 7, 9, 6, 10, 5, 11, 4, 12, 3, 13, 2, 14, 0]
AHEAD, LAG, MID_AT, MERGE_AT = 6, 3, 10, -3
MESSAGES = 76
STAGES = 4


def kernel(
    cols_in, owner_in, factor, coeffs_in, out,
    cols, owner, coeffs_t, f_buf, c_all, half, mine, tiles, by_y, by_z, place,
    s_msg, r_msg, s_scale, r_scale, kept, merged,
    arg_in, f_in, g_out, g_in, py_out, py_in, pz_out, pz_in, p_in,
    m_out, m_in, c_out, c_in,
):
    me, occ = lax.axis_index("aux"), lax.axis_index("occ")
    y, z = me // NZ, me % NZ
    x, core = occ // 2, occ % 2
    aux_count, nb, entries, blk, _ = f_buf.shape
    own, rows = out.shape[0], out.shape[1]
    share = coeffs_t.shape[0]
    all_occ = c_all.shape[1]
    step = nb // STAGES

    def up_y(k):
        return (y + k) % NY * NZ + z

    def up_z(k):
        return y * NZ + (z + k) % NZ

    def peer(dx, other_core=False):
        return (x + dx) % NX * 2 + (1 - core if other_core else core)

    args = [
        pltpu.make_async_copy(src, dst, arg_in.at[n])
        for n, (src, dst) in enumerate(((coeffs_in, coeffs_t), (owner_in, owner), (cols_in, cols)))
    ]
    for arg in args:
        arg.start()
    loads = [
        pltpu.make_async_copy(
            factor.at[:, pl.ds(n * step, step)], f_buf.at[:, pl.ds(n * step, step)], f_in.at[n]
        )
        for n in range(STAGES)
    ]
    for load in loads:
        load.start()

    barrier = pltpu.get_barrier_semaphore()
    aux_peers = [up_y(k) for k in range(1, NY)] + [up_z(k) for k in range(1, NZ)]
    occ_peers = [peer(1), peer(NX - 1), peer(0, True)]
    for other in aux_peers:
        pl.semaphore_signal(barrier, inc=1, device_id={"aux": other}, device_id_type=MESH)
    for other in occ_peers:
        pl.semaphore_signal(barrier, inc=1, device_id={"occ": other}, device_id_type=MESH)

    for arg in args:
        arg.wait()
    for b in range(nb):
        c_all[b, pl.ds(pl.multiple_of(occ * share, share), share), :] = coeffs_t[
            :, b * blk : (b + 1) * blk
        ]
    lane = lax.broadcasted_iota(jnp.int32, (1, 128), 1)
    codes = jnp.zeros((1, 128), jnp.int32)
    for t in range(own):
        pair_index = owner[t]
        codes = jnp.where(lane == t, (pair_index % nb) * nb + pair_index // nb, codes)
    by_y[y] = codes
    pl.semaphore_wait(barrier, len(aux_peers) + len(occ_peers))

    def send(src, dst, out_sem, in_sem, **other):
        return pltpu.make_async_remote_copy(
            src_ref=src, dst_ref=dst, send_sem=out_sem, recv_sem=in_sem,
            device_id=other, device_id_type=MESH,
        )

    def block(who, part):
        lo, count = (0, nb) if part is None else (part * (nb // 2), nb // 2)
        return c_all.at[pl.ds(lo, count), pl.ds(pl.multiple_of(who * share, share), share)]

    def pass_on(n, who, part, to):
        ref = block(who, part)
        return send(ref, ref, g_out.at[n], g_in.at[n], occ=to)

    right, left, mate = peer(1), peer(NX - 1), peer(0, True)
    moves = [
        (occ, peer(-1 + NX), 0, right),
        (occ, peer(1), 1, left),
        (occ, peer(-1 + NX), 1, right),
        (occ, peer(1), 0, left),
        (peer(-1 + NX), peer(2), 0, right),
        (peer(1), peer(2), 1, left),
        (occ, mate, None, mate),
        (peer(-1 + NX), peer(-1 + NX, True), 0, mate),
        (peer(1), peer(1, True), 1, mate),
        (peer(-1 + NX), peer(-1 + NX, True), 1, mate),
        (peer(1), peer(1, True), 0, mate),
        (peer(2), peer(2, True), 0, mate),
        (peer(2), peer(2, True), 1, mate),
    ]

    def go(n):
        pass_on(n, moves[n][0], moves[n][2], moves[n][3]).start()

    def got(n):
        pass_on(n, moves[n][1], moves[n][2], moves[n][3]).wait_recv()

    def place_y(k, row):
        return send(by_y.at[row], by_y.at[row], py_out.at[k - 1], py_in.at[k - 1], aux=up_y(k))

    def place_z(k, row):
        return send(by_z.at[row], by_z.at[row], pz_out.at[k - 1], pz_in.at[k - 1], aux=up_z(k))

    for n in (0, 1, 2, 3, 6):
        go(n)
    for k in range(1, NY):
        place_y(k, y).start()
    for n, then in ((0, (4, 7)), (1, (5, 8)), (2, (9,)), (3, (10,))):
        got(n)
        for nxt in then:
            go(nxt)
    for k in range(1, NY):
        place_y(k, (y + NY - k) % NY).wait_recv()
    by_z[z] = by_y[...]
    for k in range(1, NZ):
        place_z(k, z).start()
    for n, nxt in ((4, 11), (5, 12)):
        got(n)
        go(nxt)
    for n in range(6, 13):
        got(n)

    for n in range(STAGES):
        loads[n].wait()

        def one(m, carry):
            for q in range(aux_count):
                lhs = jnp.concatenate([f_buf[q, m, s] for s in range(entries)], axis=1)
                rhs = jnp.concatenate([c_all[cols[q, s, m]] for s in range(entries)], axis=1)
                done = lax.dot_general(lhs, rhs, NT, preferred_element_type=jnp.float32)
                half[m, :, q * all_occ : (q + 1) * all_occ] = done.astype(jnp.bfloat16)
            mine[m] = half[m, pl.ds(pl.multiple_of(occ * rows, rows), rows), :]
            return carry

        lax.fori_loop(n * step, (n + 1) * step, one, 0, unroll=2)

    def pair(p, carry):
        lhs = mine[...].reshape(nb * rows, aux_count * all_occ)
        rhs = half[pl.ds(2 * p, 2)].reshape(2 * blk, aux_count * all_occ)
        prod = lax.dot_general(lhs, rhs, NT, preferred_element_type=jnp.float32)
        tiles[pl.ds(2 * p * nb, nb)] = prod[:, :blk].reshape(nb, rows, blk)
        tiles[pl.ds((2 * p + 1) * nb, nb)] = prod[:, blk:].reshape(nb, rows, blk)
        return carry

    lax.fori_loop(0, nb // 2, pair, 0, unroll=2)

    for k in range(1, NZ):
        place_z(k, (z + NZ - k) % NZ).wait_recv()
    fetch = pltpu.make_async_copy(by_z, place, p_in.at[0])
    fetch.start()
    fetch.wait()

    def post(n, part, axis_to):
        top = jnp.maximum(jnp.max(jnp.abs(part), axis=0, keepdims=True), 1e-30)
        count = part.shape[0]
        s_msg[n, :count] = jnp.round(part * (32767.0 / top)).astype(jnp.int32).astype(jnp.int16)
        s_scale[n] = top * (1.0 / 32767.0)
        sent.append((n, count, axis_to))
        for copy in copies(n, count, axis_to):
            copy.start()

    def copies(n, count, axis_to):
        piece = pl.ds(0, count)
        return (
            send(s_msg.at[n, piece], r_msg.at[n, piece], m_out.at[n], m_in.at[n], aux=axis_to),
            send(s_scale.at[n], r_scale.at[n], c_out.at[n], c_in.at[n], aux=axis_to),
        )

    def take(n, count):
        for copy in copies(n, count, y_to[0]):
            copy.wait_recv()
        return r_msg[n, :count].astype(jnp.int32).astype(jnp.float32) * r_scale[n]

    sent = []
    y_to = [up_y(1), up_y(NY - 1)]
    z_to = [up_z(1), up_z(NZ - 1)]
    far_to = [up_z(4), up_z(NZ - 4)]
    size, cut = own * rows, (own + 1) // 2 * rows
    halves = (cut, size - cut)
    msg_a, msg_b, msg_n, msg_q, msg_e, msg_m = 0, 16, 48, 64, 66, 68

    def chunk(up, d):
        yy, zz = (y + up) % NY, (z + d) % NZ
        return jnp.concatenate([tiles[place[zz, yy, 0, t]] for t in range(own)], axis=0)

    def near(up, d):
        return merged[up] if d == 0 else chunk(up, d)

    def way(d):
        return 0 if 1 <= d <= NZ // 2 else 1

    def first_hop(d):
        post(msg_a + d, near(2, d), y_to[way(d)])

    def second_hop(d):
        for w, up in ((0, 1), (1, NY - 1)):
            part = near(up, d)
            if way(d) == w:
                part = part + take(msg_a + d, size)
            post(msg_b + w * NZ + d, part, y_to[w])

    def column(d):
        part = near(0, d) + take(msg_b + d, size) + take(msg_b + NZ + d, size)
        if d % 4 == 0 and d != 8:
            kept[d // 4] = part
        elif d == 8:
            post(msg_q, part[:cut], far_to[0])
            post(msg_q + 1, part[cut:], far_to[1])
        else:
            hop = d % 4 if d < 8 else -(-d % 4)
            post(msg_n + d, part, up_z(hop % NZ))

    def merge_out():
        for up in (2, 1, 3, 0):
            for w, d in ((0, 1), (1, NZ - 1)):
                post(msg_m + w * NY + up, chunk(up, d), z_to[w])

    def merge_in():
        for up in (2, 1, 3, 0):
            merged[up] = chunk(up, 0) + take(msg_m + up, size) + take(msg_m + NY + up, size)

    def collect(d, others):
        part = kept[d // 4]
        for o in others:
            part = part + take(msg_n + o, size)
        return part

    def collect_mid(w):
        part = collect(*((4, (7, 6, 5)), (12, (9, 10, 11)))[w])
        came = take(msg_q + w, halves[w])
        if w == 0:
            part = jnp.concatenate([part[:cut] + came, part[cut:]], axis=0)
        else:
            part = jnp.concatenate([part[:cut], part[cut:] + came], axis=0)
        post(msg_e + w, part, far_to[w])

    count = len(ORDER)
    for i in range(-AHEAD, count + LAG):
        if i + AHEAD < count:
            if ORDER[i + AHEAD] == 0:
                merge_in()
            first_hop(ORDER[i + AHEAD])
        if i == MERGE_AT:
            merge_out()
        if 0 <= i < count:
            second_hop(ORDER[i])
        if i - LAG >= 0:
            column(ORDER[i - LAG])
        if i - LAG == MID_AT:
            collect_mid(0)
            collect_mid(1)
    part = collect(0, (3, 13, 2, 14))
    for w in range(2):
        part = part + take(msg_e + w, size)
    out[...] = part.reshape(own, rows, blk)

    for n, count, axis_to in sent:
        for copy in copies(n, count, axis_to):
            copy.wait_send()
    for n in range(13):
        pass_on(n, moves[n][0], moves[n][2], moves[n][3]).wait_send()
    for k in range(1, NY):
        place_y(k, y).wait_send()
    for k in range(1, NZ):
        place_z(k, z).wait_send()


def shards(factor_tiles, tile_cols, coeffs, pair_owner):
    aux_count, nb, entries, blk, _ = factor_tiles.shape
    occ_ways = lax.axis_size("occ")
    rows = blk // occ_ways
    occ = coeffs.shape[1] * occ_ways
    own = pair_owner.shape[0]
    dma = pltpu.SemaphoreType.DMA
    vmem = pl.BlockSpec(memory_space=pltpu.VMEM)
    return pl.pallas_call(
        kernel,
        in_specs=[pl.BlockSpec(memory_space=pltpu.HBM)] * 4,
        out_specs=vmem,
        out_shape=jax.ShapeDtypeStruct((own, rows, blk), jnp.float32),
        scratch_shapes=[
            pltpu.SMEM((aux_count, entries, nb), jnp.int32),
            pltpu.SMEM((own,), jnp.int32),
            pltpu.VMEM(coeffs.shape[::-1], jnp.bfloat16),
            pltpu.VMEM(factor_tiles.shape, jnp.bfloat16),
            pltpu.VMEM((nb, occ, blk), jnp.bfloat16),
            pltpu.VMEM((nb, blk, aux_count * occ), jnp.bfloat16),
            pltpu.VMEM((nb, rows, aux_count * occ), jnp.bfloat16),
            pltpu.VMEM((nb * nb, rows, blk), jnp.float32),
            pltpu.VMEM((NY, 1, 128), jnp.int32),
            pltpu.VMEM((NZ, NY, 1, 128), jnp.int32),
            pltpu.SMEM((NZ, NY, 1, 128), jnp.int32),
            pltpu.VMEM((MESSAGES, own * rows, blk), jnp.int16),
            pltpu.VMEM((MESSAGES, own * rows, blk), jnp.int16),
            pltpu.VMEM((MESSAGES, 1, blk), jnp.float32),
            pltpu.VMEM((MESSAGES, 1, blk), jnp.float32),
            pltpu.VMEM((4, own * rows, blk), jnp.float32),
            pltpu.VMEM((NY, own * rows, blk), jnp.float32),
            dma((3,)),
            dma((STAGES,)),
            dma((13,)), dma((13,)),
            dma((NY - 1,)), dma((NY - 1,)),
            dma((NZ - 1,)), dma((NZ - 1,)),
            dma((1,)),
            dma((MESSAGES,)), dma((MESSAGES,)),
            dma((MESSAGES,)), dma((MESSAGES,)),
        ],
        compiler_params=pltpu.CompilerParams(
            collective_id=0, has_side_effects=True, vmem_limit_bytes=61 * 2**20
        ),
    )(jnp.transpose(tile_cols, (0, 2, 1)), pair_owner, factor_tiles, coeffs.T)


def solution(mesh):
    placed = (P("aux", None, None, None, None), P("aux", None, None), P(None, "occ"), P("aux"))
    return jax.shard_map(
        shards, mesh=mesh, in_specs=placed, out_specs=P("aux", "occ", None), check_vma=False
    )
```

```python
import jax
import jax.numpy as jnp
from jax import lax
from jax.experimental import pallas as pl
from jax.experimental.pallas import tpu as pltpu
from jax.sharding import PartitionSpec as P

NT = (((1,), (1,)), ((), ()))
NX, NY, NZ = 4, 4, 16
MESH = pl.DeviceIdType.MESH
ORDER = [8, 7, 9, 6, 10, 5, 11, 4, 12, 3, 13, 2, 14, 0]
AHEAD, LAG, MID_AT, MERGE_AT, LATE_BY = 13, 7, 11, -9, 6
MESSAGES = 76
STAGES = 4


def kernel(
    cols_in, owner_in, factor, coeffs_in, out,
    cols, owner, coeffs_t, f_buf, c_near, c_far, half, mine, tiles, by_y, by_z, place,
    s_msg, r_msg, s_scale, r_scale, kept, merged,
    arg_in, f_in, g_out, g_in, py_out, py_in, pz_out, pz_in, p_in,
    m_out, m_in, c_out, c_in,
):
    me, occ = lax.axis_index("aux"), lax.axis_index("occ")
    y, z = me // NZ, me % NZ
    x, core = occ // 2, occ % 2
    aux_count, nb, entries, blk, _ = f_buf.shape
    own, rows = out.shape[0], out.shape[1]
    share = coeffs_t.shape[0]
    lanes = c_near.shape[1]
    all_occ = 2 * lanes
    step = nb // STAGES

    def up_y(k):
        return (y + k) % NY * NZ + z

    def up_z(k):
        return y * NZ + (z + k) % NZ

    def peer(dx, other_core=False):
        return (x + dx) % NX * 2 + (1 - core if other_core else core)

    args = [
        pltpu.make_async_copy(src, dst, arg_in.at[n])
        for n, (src, dst) in enumerate(((coeffs_in, coeffs_t), (owner_in, owner), (cols_in, cols)))
    ]
    for arg in args:
        arg.start()
    loads = [
        pltpu.make_async_copy(
            factor.at[:, pl.ds(n * step, step)], f_buf.at[:, pl.ds(n * step, step)], f_in.at[n]
        )
        for n in range(STAGES)
    ]
    for load in loads:
        load.start()

    barrier = pltpu.get_barrier_semaphore()
    aux_peers = [up_y(k) for k in range(1, NY)] + [up_z(k) for k in range(1, NZ)]
    occ_peers = [peer(1), peer(NX - 1), peer(0, True)]
    for other in aux_peers:
        pl.semaphore_signal(barrier, inc=1, device_id={"aux": other}, device_id_type=MESH)
    for other in occ_peers:
        pl.semaphore_signal(barrier, inc=1, device_id={"occ": other}, device_id_type=MESH)

    for arg in args:
        arg.wait()
    for b in range(nb):
        c_near[b, :share, :] = coeffs_t[:, b * blk : (b + 1) * blk]
    lane = lax.broadcasted_iota(jnp.int32, (1, 128), 1)
    codes = jnp.zeros((1, 128), jnp.int32)
    for t in range(own):
        pair_index = owner[t]
        codes = jnp.where(lane == t, (pair_index % nb) * nb + pair_index // nb, codes)
    by_y[y] = codes
    pl.semaphore_wait(barrier, len(aux_peers) + len(occ_peers))

    def send(src, dst, out_sem, in_sem, **other):
        return pltpu.make_async_remote_copy(
            src_ref=src, dst_ref=dst, send_sem=out_sem, recv_sem=in_sem,
            device_id=other, device_id_type=MESH,
        )

    def block(slot, part):
        lo, count = (0, nb) if part is None else (part * (nb // 2), nb // 2)
        ref, at = (c_near, slot) if slot < 4 else (c_far, slot - 4)
        return ref.at[pl.ds(lo, count), pl.ds(at * share, share)]

    def pass_on(n):
        src, dst, part, to = moves[n]
        return send(block(src, part), block(dst, part), g_out.at[n], g_in.at[n], occ=to)

    right, left, mate = peer(1), peer(NX - 1), peer(0, True)
    moves = [
        (0, 2, 0, right),
        (0, 4, 1, left),
        (0, 2, 1, right),
        (0, 4, 0, left),
        (2, 6, 0, right),
        (4, 6, 1, left),
        (0, 1, None, mate),
        (2, 3, 0, mate),
        (4, 5, 1, mate),
        (2, 3, 1, mate),
        (4, 5, 0, mate),
        (6, 7, 0, mate),
        (6, 7, 1, mate),
    ]

    def go(n):
        pass_on(n).start()

    def got(n):
        pass_on(n).wait_recv()

    def place_y(k, row):
        return send(by_y.at[row], by_y.at[row], py_out.at[k - 1], py_in.at[k - 1], aux=up_y(k))

    def place_z(k, row):
        return send(by_z.at[row], by_z.at[row], pz_out.at[k - 1], pz_in.at[k - 1], aux=up_z(k))

    for n in (0, 1, 2, 3, 6):
        go(n)
    for k in range(1, NY):
        place_y(k, y).start()
    for n, then in ((0, (4, 7)), (1, (5, 8)), (2, (9,)), (3, (10,))):
        got(n)
        for nxt in then:
            go(nxt)
    for k in range(1, NY):
        place_y(k, (y + NY - k) % NY).wait_recv()
    by_z[z] = by_y[...]
    for k in range(1, NZ):
        place_z(k, z).start()
    def halves_of(first, last, side, finish):
        def one(m, carry):
            for q in range(aux_count):
                lhs = jnp.concatenate([f_buf[q, m, s] for s in range(entries)], axis=1)
                blocks = c_far if side else c_near
                rhs = jnp.concatenate([blocks[cols[q, s, m]] for s in range(entries)], axis=1)
                done = lax.dot_general(lhs, rhs, NT, preferred_element_type=jnp.float32)
                at = q * all_occ + side * lanes
                half[m, :, at : at + lanes] = done.astype(jnp.bfloat16)
            if finish:
                mine[m] = half[m, pl.ds(pl.multiple_of(occ * rows, rows), rows), :]
            return carry

        lax.fori_loop(first, last, one, 0, unroll=6)

    for load in loads:
        load.wait()
    for n in (6, 7, 9):
        got(n)
    halves_of(0, nb // 4, 0, False)
    for n, nxt in ((4, 11), (5, 12)):
        got(n)
        go(nxt)
    halves_of(nb // 4, nb, 0, False)
    for n in (8, 10, 11, 12):
        got(n)
    halves_of(0, nb, 1, True)

    for k in range(1, NZ):
        place_z(k, (z + NZ - k) % NZ).wait_recv()
    fetch = pltpu.make_async_copy(by_z, place, p_in.at[0])
    fetch.start()

    def pair(p, carry):
        lhs = mine[...].reshape(nb * rows, aux_count * all_occ)
        rhs = half[pl.ds(2 * p, 2)].reshape(2 * blk, aux_count * all_occ)
        prod = lax.dot_general(lhs, rhs, NT, preferred_element_type=jnp.float32)
        tiles[pl.ds(2 * p * nb, nb)] = prod[:, :blk].reshape(nb, rows, blk)
        tiles[pl.ds((2 * p + 1) * nb, nb)] = prod[:, blk:].reshape(nb, rows, blk)
        return carry

    lax.fori_loop(0, nb // 2, pair, 0, unroll=6)

    fetch.wait()

    def post(n, part, axis_to):
        top = jnp.maximum(jnp.max(jnp.abs(part), axis=0, keepdims=True), 1e-30)
        count = part.shape[0]
        s_msg[n, :count] = jnp.round(part * (32767.0 / top)).astype(jnp.int32).astype(jnp.int16)
        s_scale[n] = top * (1.0 / 32767.0)
        sent.append((n, count, axis_to))
        for copy in copies(n, count, axis_to):
            copy.start()

    def copies(n, count, axis_to):
        piece = pl.ds(0, count)
        return (
            send(s_msg.at[n, piece], r_msg.at[n, piece], m_out.at[n], m_in.at[n], aux=axis_to),
            send(s_scale.at[n], r_scale.at[n], c_out.at[n], c_in.at[n], aux=axis_to),
        )

    def take(n, count):
        for copy in copies(n, count, y_to[0]):
            copy.wait_recv()
        return r_msg[n, :count].astype(jnp.int32).astype(jnp.float32) * r_scale[n]

    sent = []
    y_to = [up_y(1), up_y(NY - 1)]
    z_to = [up_z(1), up_z(NZ - 1)]
    far_to = [up_z(4), up_z(NZ - 4)]
    size, cut = own * rows, (own + 1) // 2 * rows
    halves = (cut, size - cut)
    msg_a, msg_b, msg_n, msg_q, msg_e, msg_m = 0, 16, 48, 64, 66, 68

    def chunk(up, d):
        yy, zz = (y + up) % NY, (z + d) % NZ
        return jnp.concatenate([tiles[place[zz, yy, 0, t]] for t in range(own)], axis=0)

    def near(up, d):
        return merged[up] if d == 0 else chunk(up, d)

    def way(d):
        return 0 if 1 <= d <= NZ // 2 else 1

    def first_hop(d):
        post(msg_a + d, near(2, d), y_to[way(d)])

    def second_hop(d):
        for w, up in ((0, 1), (1, NY - 1)):
            part = near(up, d)
            if way(d) == w:
                part = part + take(msg_a + d, size)
            post(msg_b + w * NZ + d, part, y_to[w])

    def column(d):
        part = near(0, d) + take(msg_b + d, size) + take(msg_b + NZ + d, size)
        if d % 4 == 0 and d != 8:
            kept[d // 4] = part
        elif d == 8:
            post(msg_q, part[:cut], far_to[0])
            post(msg_q + 1, part[cut:], far_to[1])
        else:
            hop = d % 4 if d < 8 else -(-d % 4)
            post(msg_n + d, part, up_z(hop % NZ))

    def merge_out():
        for up in (2, 1, 3, 0):
            for w, d in ((0, 1), (1, NZ - 1)):
                post(msg_m + w * NY + up, chunk(up, d), z_to[w])

    def merge_in():
        for up in (2, 1, 3, 0):
            merged[up] = chunk(up, 0) + take(msg_m + up, size) + take(msg_m + NY + up, size)

    def collect(d, others):
        part = kept[d // 4]
        for o in others:
            part = part + take(msg_n + o, size)
        return part

    def collect_mid(w):
        part = collect(*((4, (7, 6, 5)), (12, (9, 10, 11)))[w])
        came = take(msg_q + w, halves[w])
        if w == 0:
            part = jnp.concatenate([part[:cut] + came, part[cut:]], axis=0)
        else:
            part = jnp.concatenate([part[:cut], part[cut:] + came], axis=0)
        post(msg_e + w, part, far_to[w])

    count = len(ORDER)
    for i in range(-AHEAD, count + LAG):
        if i + AHEAD < count - 1:
            first_hop(ORDER[i + AHEAD])
        if i == MERGE_AT:
            merge_out()
        if i == count - 1 - LATE_BY:
            merge_in()
            first_hop(ORDER[-1])
        if 0 <= i < count:
            second_hop(ORDER[i])
        if i - LAG >= 0:
            column(ORDER[i - LAG])
        if i - LAG == MID_AT:
            collect_mid(0)
            collect_mid(1)
    part = collect(0, (3, 13, 2, 14))
    for w in range(2):
        part = part + take(msg_e + w, size)
    out[...] = part.reshape(own, rows, blk)

    for n, count, axis_to in sent:
        for copy in copies(n, count, axis_to):
            copy.wait_send()
    for n in range(13):
        pass_on(n).wait_send()
    for k in range(1, NY):
        place_y(k, y).wait_send()
    for k in range(1, NZ):
        place_z(k, z).wait_send()


def shards(factor_tiles, tile_cols, coeffs, pair_owner):
    aux_count, nb, entries, blk, _ = factor_tiles.shape
    occ_ways = lax.axis_size("occ")
    rows = blk // occ_ways
    occ = coeffs.shape[1] * occ_ways
    own = pair_owner.shape[0]
    dma = pltpu.SemaphoreType.DMA
    vmem = pl.BlockSpec(memory_space=pltpu.VMEM)
    return pl.pallas_call(
        kernel,
        in_specs=[pl.BlockSpec(memory_space=pltpu.HBM)] * 4,
        out_specs=vmem,
        out_shape=jax.ShapeDtypeStruct((own, rows, blk), jnp.float32),
        scratch_shapes=[
            pltpu.SMEM((aux_count, entries, nb), jnp.int32),
            pltpu.SMEM((own,), jnp.int32),
            pltpu.VMEM(coeffs.shape[::-1], jnp.bfloat16),
            pltpu.VMEM(factor_tiles.shape, jnp.bfloat16),
            pltpu.VMEM((nb, occ // 2, blk), jnp.bfloat16),
            pltpu.VMEM((nb, occ // 2, blk), jnp.bfloat16),
            pltpu.VMEM((nb, blk, aux_count * occ), jnp.bfloat16),
            pltpu.VMEM((nb, rows, aux_count * occ), jnp.bfloat16),
            pltpu.VMEM((nb * nb, rows, blk), jnp.float32),
            pltpu.VMEM((NY, 1, 128), jnp.int32),
            pltpu.VMEM((NZ, NY, 1, 128), jnp.int32),
            pltpu.SMEM((NZ, NY, 1, 128), jnp.int32),
            pltpu.VMEM((MESSAGES, own * rows, blk), jnp.int16),
            pltpu.VMEM((MESSAGES, own * rows, blk), jnp.int16),
            pltpu.VMEM((MESSAGES, 1, blk), jnp.float32),
            pltpu.VMEM((MESSAGES, 1, blk), jnp.float32),
            pltpu.VMEM((4, own * rows, blk), jnp.float32),
            pltpu.VMEM((NY, own * rows, blk), jnp.float32),
            dma((3,)),
            dma((STAGES,)),
            dma((13,)), dma((13,)),
            dma((NY - 1,)), dma((NY - 1,)),
            dma((NZ - 1,)), dma((NZ - 1,)),
            dma((1,)),
            dma((MESSAGES,)), dma((MESSAGES,)),
            dma((MESSAGES,)), dma((MESSAGES,)),
        ],
        compiler_params=pltpu.CompilerParams(
            collective_id=0, has_side_effects=True, vmem_limit_bytes=61 * 2**20
        ),
    )(jnp.transpose(tile_cols, (0, 2, 1)), pair_owner, factor_tiles, coeffs.T)


def solution(mesh):
    placed = (P("aux", None, None, None, None), P("aux", None, None), P(None, "occ"), P("aux"))
    return jax.shard_map(
        shards, mesh=mesh, in_specs=placed, out_specs=P("aux", "occ", None), check_vma=False
    )
```

```python
import jax
import jax.numpy as jnp
from jax import lax
from jax.experimental import pallas as pl
from jax.experimental.pallas import tpu as pltpu
from jax.sharding import PartitionSpec as P

NT = (((1,), (1,)), ((), ()))
NX, NY, NZ = 4, 4, 16
MESH = pl.DeviceIdType.MESH
ORDER = [8, 7, 9, 6, 10, 5, 11, 4, 12, 3, 13, 2, 14, 0]
AHEAD, LAG, MID_AT, MERGE_AT, LATE_BY = 13, 7, 11, -9, 6
MESSAGES = 76
STAGES = 4


def kernel(
    cols_in, owner_in, factor, coeffs_in, out,
    cols, owner, coeffs_t, f_buf, c_near, c_far, half, mine, tiles, by_y, by_z, place,
    s_msg, r_msg, s_scale, r_scale, kept, merged,
    arg_in, f_in, g_out, g_in, py_out, py_in, pz_out, pz_in, p_in,
    m_out, m_in, c_out, c_in,
):
    me, occ = lax.axis_index("aux"), lax.axis_index("occ")
    y, z = me // NZ, me % NZ
    x, core = occ // 2, occ % 2
    aux_count, nb, entries, blk, _ = f_buf.shape
    own, rows = out.shape[0], out.shape[1]
    share = coeffs_t.shape[0]
    lanes = c_near.shape[1]
    all_occ = 2 * lanes
    step = nb // STAGES

    def up_y(k):
        return (y + k) % NY * NZ + z

    def up_z(k):
        return y * NZ + (z + k) % NZ

    def peer(dx, other_core=False):
        return (x + dx) % NX * 2 + (1 - core if other_core else core)

    args = [
        pltpu.make_async_copy(src, dst, arg_in.at[n])
        for n, (src, dst) in enumerate(((coeffs_in, coeffs_t), (owner_in, owner), (cols_in, cols)))
    ]
    for arg in args:
        arg.start()
    loads = [
        pltpu.make_async_copy(
            factor.at[:, pl.ds(n * step, step)], f_buf.at[:, pl.ds(n * step, step)], f_in.at[n]
        )
        for n in range(STAGES)
    ]
    for load in loads:
        load.start()

    barrier = pltpu.get_barrier_semaphore()
    reach = [1, 2, 3, 4, NZ - 1, NZ - 2, NZ - 3, NZ - 4]
    aux_peers = [up_y(k) for k in range(1, NY)] + [up_z(k) for k in reach]
    occ_peers = [peer(1), peer(NX - 1), peer(0, True)]
    for other in aux_peers:
        pl.semaphore_signal(barrier, inc=1, device_id={"aux": other}, device_id_type=MESH)
    for other in occ_peers:
        pl.semaphore_signal(barrier, inc=1, device_id={"occ": other}, device_id_type=MESH)

    for arg in args:
        arg.wait()
    for b in range(nb):
        c_near[b, :share, :] = coeffs_t[:, b * blk : (b + 1) * blk]
    lane = lax.broadcasted_iota(jnp.int32, (1, 128), 1)
    codes = jnp.zeros((1, 128), jnp.int32)
    for t in range(own):
        pair_index = owner[t]
        codes = jnp.where(lane == t, (pair_index % nb) * nb + pair_index // nb, codes)
    by_y[y] = codes
    pl.semaphore_wait(barrier, len(aux_peers) + len(occ_peers))

    def send(src, dst, out_sem, in_sem, **other):
        return pltpu.make_async_remote_copy(
            src_ref=src, dst_ref=dst, send_sem=out_sem, recv_sem=in_sem,
            device_id=other, device_id_type=MESH,
        )

    def block(slot, part):
        lo, count = (0, nb) if part is None else (part * (nb // 2), nb // 2)
        ref, at = (c_near, slot) if slot < 4 else (c_far, slot - 4)
        return ref.at[pl.ds(lo, count), pl.ds(at * share, share)]

    def pass_on(n):
        src, dst, part, to = moves[n]
        return send(block(src, part), block(dst, part), g_out.at[n], g_in.at[n], occ=to)

    right, left, mate = peer(1), peer(NX - 1), peer(0, True)
    moves = [
        (0, 2, 0, right),
        (0, 4, 1, left),
        (0, 2, 1, right),
        (0, 4, 0, left),
        (2, 6, 0, right),
        (4, 6, 1, left),
        (0, 1, None, mate),
        (2, 3, 0, mate),
        (4, 5, 1, mate),
        (2, 3, 1, mate),
        (4, 5, 0, mate),
        (6, 7, 0, mate),
        (6, 7, 1, mate),
    ]

    def go(n):
        pass_on(n).start()

    def got(n):
        pass_on(n).wait_recv()

    def place_y(k, row):
        return send(by_y.at[row], by_y.at[row], py_out.at[k - 1], py_in.at[k - 1], aux=up_y(k))

    rounds = [(k, 0) for k in reach]
    rounds += [(4, NZ - k) for k in range(1, 5)] + [(NZ - 4, k) for k in range(1, 4)]

    def place_z(n, receiving=False):
        far, whose = rounds[n]
        slot = (z + whose + (NZ - far if receiving else 0)) % NZ
        return send(by_z.at[slot], by_z.at[slot], pz_out.at[n], pz_in.at[n], aux=up_z(far))

    for n in (0, 1, 2, 3, 6):
        go(n)
    for k in range(1, NY):
        place_y(k, y).start()
    for n, then in ((0, (4, 7)), (1, (5, 8)), (2, (9,)), (3, (10,))):
        got(n)
        for nxt in then:
            go(nxt)
    for k in range(1, NY):
        place_y(k, (y + NY - k) % NY).wait_recv()
    by_z[z] = by_y[...]
    for n in range(len(reach)):
        place_z(n).start()
    def halves_of(first, last, side, finish):
        def one(m, carry):
            for q in range(aux_count):
                lhs = jnp.concatenate([f_buf[q, m, s] for s in range(entries)], axis=1)
                blocks = c_far if side else c_near
                rhs = jnp.concatenate([blocks[cols[q, s, m]] for s in range(entries)], axis=1)
                done = lax.dot_general(lhs, rhs, NT, preferred_element_type=jnp.float32)
                at = q * all_occ + side * lanes
                half[m, :, at : at + lanes] = done.astype(jnp.bfloat16)
            if finish:
                mine[m] = half[m, pl.ds(pl.multiple_of(occ * rows, rows), rows), :]
            return carry

        lax.fori_loop(first, last, one, 0, unroll=6)

    for load in loads:
        load.wait()
    for n in (6, 7, 9):
        got(n)
    halves_of(0, nb // 4, 0, False)
    for n, nxt in ((4, 11), (5, 12)):
        got(n)
        go(nxt)
    for n in range(len(reach)):
        place_z(n, True).wait_recv()
    for n in range(len(reach), len(rounds)):
        place_z(n).start()
    halves_of(nb // 4, nb, 0, False)
    for n in (8, 10, 11, 12):
        got(n)
    halves_of(0, nb, 1, True)

    for n in range(len(reach), len(rounds)):
        place_z(n, True).wait_recv()
    fetch = pltpu.make_async_copy(by_z, place, p_in.at[0])
    fetch.start()

    def pair(p, carry):
        lhs = mine[...].reshape(nb * rows, aux_count * all_occ)
        rhs = half[pl.ds(2 * p, 2)].reshape(2 * blk, aux_count * all_occ)
        prod = lax.dot_general(lhs, rhs, NT, preferred_element_type=jnp.float32)
        tiles[pl.ds(2 * p * nb, nb)] = prod[:, :blk].reshape(nb, rows, blk)
        tiles[pl.ds((2 * p + 1) * nb, nb)] = prod[:, blk:].reshape(nb, rows, blk)
        return carry

    lax.fori_loop(0, nb // 2, pair, 0, unroll=6)

    fetch.wait()

    def post(n, part, axis_to):
        top = jnp.maximum(jnp.max(jnp.abs(part), axis=0, keepdims=True), 1e-30)
        count = part.shape[0]
        s_msg[n, :count] = jnp.round(part * (32767.0 / top)).astype(jnp.int32).astype(jnp.int16)
        s_scale[n] = top * (1.0 / 32767.0)
        sent.append((n, count, axis_to))
        for copy in copies(n, count, axis_to):
            copy.start()

    def copies(n, count, axis_to):
        piece = pl.ds(0, count)
        return (
            send(s_msg.at[n, piece], r_msg.at[n, piece], m_out.at[n], m_in.at[n], aux=axis_to),
            send(s_scale.at[n], r_scale.at[n], c_out.at[n], c_in.at[n], aux=axis_to),
        )

    def take(n, count):
        for copy in copies(n, count, y_to[0]):
            copy.wait_recv()
        return r_msg[n, :count].astype(jnp.int32).astype(jnp.float32) * r_scale[n]

    sent = []
    y_to = [up_y(1), up_y(NY - 1)]
    z_to = [up_z(1), up_z(NZ - 1)]
    far_to = [up_z(4), up_z(NZ - 4)]
    size, cut = own * rows, (own + 1) // 2 * rows
    halves = (cut, size - cut)
    msg_a, msg_b, msg_n, msg_q, msg_e, msg_m = 0, 16, 48, 64, 66, 68

    def chunk(up, d):
        yy, zz = (y + up) % NY, (z + d) % NZ
        return jnp.concatenate([tiles[place[zz, yy, 0, t]] for t in range(own)], axis=0)

    def near(up, d):
        return merged[up] if d == 0 else chunk(up, d)

    def way(d):
        return 0 if 1 <= d <= NZ // 2 else 1

    def first_hop(d):
        post(msg_a + d, near(2, d), y_to[way(d)])

    def second_hop(d):
        for w, up in ((0, 1), (1, NY - 1)):
            part = near(up, d)
            if way(d) == w:
                part = part + take(msg_a + d, size)
            post(msg_b + w * NZ + d, part, y_to[w])

    def column(d):
        part = near(0, d) + take(msg_b + d, size) + take(msg_b + NZ + d, size)
        if d % 4 == 0 and d != 8:
            kept[d // 4] = part
        elif d == 8:
            post(msg_q, part[:cut], far_to[0])
            post(msg_q + 1, part[cut:], far_to[1])
        else:
            hop = d % 4 if d < 8 else -(-d % 4)
            post(msg_n + d, part, up_z(hop % NZ))

    def merge_out():
        for up in (2, 1, 3, 0):
            for w, d in ((0, 1), (1, NZ - 1)):
                post(msg_m + w * NY + up, chunk(up, d), z_to[w])

    def merge_in():
        for up in (2, 1, 3, 0):
            merged[up] = chunk(up, 0) + take(msg_m + up, size) + take(msg_m + NY + up, size)

    def collect(d, others):
        part = kept[d // 4]
        for o in others:
            part = part + take(msg_n + o, size)
        return part

    def collect_mid(w):
        part = collect(*((4, (7, 6, 5)), (12, (9, 10, 11)))[w])
        came = take(msg_q + w, halves[w])
        if w == 0:
            part = jnp.concatenate([part[:cut] + came, part[cut:]], axis=0)
        else:
            part = jnp.concatenate([part[:cut], part[cut:] + came], axis=0)
        post(msg_e + w, part, far_to[w])

    count = len(ORDER)
    for i in range(-AHEAD, count + LAG):
        if i + AHEAD < count - 1:
            first_hop(ORDER[i + AHEAD])
        if i == MERGE_AT:
            merge_out()
        if i == count - 1 - LATE_BY:
            merge_in()
            first_hop(ORDER[-1])
        if 0 <= i < count:
            second_hop(ORDER[i])
        if i - LAG >= 0:
            column(ORDER[i - LAG])
        if i - LAG == MID_AT:
            collect_mid(0)
            collect_mid(1)
    part = collect(0, (3, 13, 2, 14))
    for w in range(2):
        part = part + take(msg_e + w, size)
    out[...] = part.reshape(own, rows, blk)

    for n, count, axis_to in sent:
        for copy in copies(n, count, axis_to):
            copy.wait_send()
    for n in range(13):
        pass_on(n).wait_send()
    for k in range(1, NY):
        place_y(k, y).wait_send()
    for n in range(len(rounds)):
        place_z(n).wait_send()


def shards(factor_tiles, tile_cols, coeffs, pair_owner):
    aux_count, nb, entries, blk, _ = factor_tiles.shape
    occ_ways = lax.axis_size("occ")
    rows = blk // occ_ways
    occ = coeffs.shape[1] * occ_ways
    own = pair_owner.shape[0]
    dma = pltpu.SemaphoreType.DMA
    vmem = pl.BlockSpec(memory_space=pltpu.VMEM)
    return pl.pallas_call(
        kernel,
        in_specs=[pl.BlockSpec(memory_space=pltpu.HBM)] * 4,
        out_specs=vmem,
        out_shape=jax.ShapeDtypeStruct((own, rows, blk), jnp.float32),
        scratch_shapes=[
            pltpu.SMEM((aux_count, entries, nb), jnp.int32),
            pltpu.SMEM((own,), jnp.int32),
            pltpu.VMEM(coeffs.shape[::-1], jnp.bfloat16),
            pltpu.VMEM(factor_tiles.shape, jnp.bfloat16),
            pltpu.VMEM((nb, occ // 2, blk), jnp.bfloat16),
            pltpu.VMEM((nb, occ // 2, blk), jnp.bfloat16),
            pltpu.VMEM((nb, blk, aux_count * occ), jnp.bfloat16),
            pltpu.VMEM((nb, rows, aux_count * occ), jnp.bfloat16),
            pltpu.VMEM((nb * nb, rows, blk), jnp.float32),
            pltpu.VMEM((NY, 1, 128), jnp.int32),
            pltpu.VMEM((NZ, NY, 1, 128), jnp.int32),
            pltpu.SMEM((NZ, NY, 1, 128), jnp.int32),
            pltpu.VMEM((MESSAGES, own * rows, blk), jnp.int16),
            pltpu.VMEM((MESSAGES, own * rows, blk), jnp.int16),
            pltpu.VMEM((MESSAGES, 1, blk), jnp.float32),
            pltpu.VMEM((MESSAGES, 1, blk), jnp.float32),
            pltpu.VMEM((4, own * rows, blk), jnp.float32),
            pltpu.VMEM((NY, own * rows, blk), jnp.float32),
            dma((3,)),
            dma((STAGES,)),
            dma((13,)), dma((13,)),
            dma((NY - 1,)), dma((NY - 1,)),
            dma((NZ - 1,)), dma((NZ - 1,)),
            dma((1,)),
            dma((MESSAGES,)), dma((MESSAGES,)),
            dma((MESSAGES,)), dma((MESSAGES,)),
        ],
        compiler_params=pltpu.CompilerParams(
            collective_id=0, has_side_effects=True, vmem_limit_bytes=61 * 2**20
        ),
    )(jnp.transpose(tile_cols, (0, 2, 1)), pair_owner, factor_tiles, coeffs.T)


def solution(mesh):
    placed = (P("aux", None, None, None, None), P("aux", None, None), P(None, "occ"), P("aux"))
    return jax.shard_map(
        shards, mesh=mesh, in_specs=placed, out_specs=P("aux", "occ", None), check_vma=False
    )
```

```python
import jax
import jax.numpy as jnp
from jax import lax
from jax.experimental import pallas as pl
from jax.experimental.pallas import tpu as pltpu
from jax.sharding import PartitionSpec as P

NT = (((1,), (1,)), ((), ()))
NX, NY, NZ = 4, 4, 16
MESH = pl.DeviceIdType.MESH
ORDER = [8, 7, 9, 6, 10, 5, 11, 4, 12, 3, 13, 2, 14, 0]
AHEAD, LAG, MID_AT, MERGE_AT, LATE_BY = 13, 5, 10, -12, 5
MESSAGES = 76
STAGES = 4


def kernel(
    cols_in, owner_in, factor, coeffs_in, out,
    cols, owner, coeffs_t, f_buf, c_near, c_far, half, mine, tiles, by_y, by_z, place,
    s_msg, r_msg, s_scale, r_scale, kept, merged,
    arg_in, f_in, g_out, g_in, py_out, py_in, pz_out, pz_in, p_in,
    m_out, m_in, c_out, c_in,
):
    me, occ = lax.axis_index("aux"), lax.axis_index("occ")
    y, z = me // NZ, me % NZ
    x, core = occ // 2, occ % 2
    aux_count, nb, entries, blk, _ = f_buf.shape
    own, rows = out.shape[0], out.shape[1]
    share = coeffs_t.shape[0]
    lanes = c_near.shape[1]
    all_occ = 2 * lanes
    step = nb // STAGES

    def up_y(k):
        return (y + k) % NY * NZ + z

    def up_z(k):
        return y * NZ + (z + k) % NZ

    def peer(dx, other_core=False):
        return (x + dx) % NX * 2 + (1 - core if other_core else core)

    args = [
        pltpu.make_async_copy(src, dst, arg_in.at[n])
        for n, (src, dst) in enumerate(((coeffs_in, coeffs_t), (owner_in, owner), (cols_in, cols)))
    ]
    for arg in args:
        arg.start()
    loads = [
        pltpu.make_async_copy(
            factor.at[:, pl.ds(n * step, step)], f_buf.at[:, pl.ds(n * step, step)], f_in.at[n]
        )
        for n in range(STAGES)
    ]
    for load in loads:
        load.start()

    barrier = pltpu.get_barrier_semaphore()
    reach = [1, 2, 3, 4, NZ - 1, NZ - 2, NZ - 3, NZ - 4]
    aux_peers = [up_y(k) for k in range(1, NY)] + [up_z(k) for k in reach]
    occ_peers = [peer(1), peer(NX - 1), peer(0, True)]
    for other in aux_peers:
        pl.semaphore_signal(barrier, inc=1, device_id={"aux": other}, device_id_type=MESH)
    for other in occ_peers:
        pl.semaphore_signal(barrier, inc=1, device_id={"occ": other}, device_id_type=MESH)

    for arg in args:
        arg.wait()
    for b in range(nb):
        c_near[b, :share, :] = coeffs_t[:, b * blk : (b + 1) * blk]
    lane = lax.broadcasted_iota(jnp.int32, (1, 128), 1)
    codes = jnp.zeros((1, 128), jnp.int32)
    for t in range(own):
        pair_index = owner[t]
        codes = jnp.where(lane == t, (pair_index % nb) * nb + pair_index // nb, codes)
    by_y[y] = codes
    pl.semaphore_wait(barrier, len(aux_peers) + len(occ_peers))

    def send(src, dst, out_sem, in_sem, **other):
        return pltpu.make_async_remote_copy(
            src_ref=src, dst_ref=dst, send_sem=out_sem, recv_sem=in_sem,
            device_id=other, device_id_type=MESH,
        )

    def block(slot, part):
        lo, count = part[0] * (nb // 4), part[1] * (nb // 4)
        ref, at = (c_near, slot) if slot < 4 else (c_far, slot - 4)
        return ref.at[pl.ds(lo, count), pl.ds(at * share, share)]

    def pass_on(n):
        src, dst, part, to = moves[n]
        return send(block(src, part), block(dst, part), g_out.at[n], g_in.at[n], occ=to)

    right, left, mate = peer(1), peer(NX - 1), peer(0, True)
    moves = [
        (0, 2, (0, 1), right),
        (0, 4, (2, 1), left),
        (0, 2, (1, 1), right),
        (0, 4, (3, 1), left),
        (0, 2, (2, 2), right),
        (0, 4, (0, 2), left),
        (0, 1, (0, 4), mate),
        (2, 6, (0, 1), right),
        (4, 6, (2, 1), left),
        (2, 6, (1, 1), right),
        (4, 6, (3, 1), left),
        (2, 3, (0, 2), mate),
        (4, 5, (2, 2), mate),
        (2, 3, (2, 2), mate),
        (4, 5, (0, 2), mate),
        (6, 7, (0, 1), mate),
        (6, 7, (2, 1), mate),
        (6, 7, (1, 1), mate),
        (6, 7, (3, 1), mate),
    ]

    def go(n):
        pass_on(n).start()

    def got(n):
        pass_on(n).wait_recv()

    def place_y(k, row):
        return send(by_y.at[row], by_y.at[row], py_out.at[k - 1], py_in.at[k - 1], aux=up_y(k))

    rounds = [(k, 0) for k in reach]
    rounds += [(4, NZ - k) for k in range(1, 5)] + [(NZ - 4, k) for k in range(1, 4)]

    def place_z(n, receiving=False):
        far, whose = rounds[n]
        slot = (z + whose + (NZ - far if receiving else 0)) % NZ
        return send(by_z.at[slot], by_z.at[slot], pz_out.at[n], pz_in.at[n], aux=up_z(far))

    for n in range(7):
        go(n)
    for k in range(1, NY):
        place_y(k, y).start()
    for n, then in ((0, (7,)), (1, (8,)), (2, (9, 11)), (3, (10, 12)), (4, (13,)), (5, (14,))):
        got(n)
        for nxt in then:
            go(nxt)
    for k in range(1, NY):
        place_y(k, (y + NY - k) % NY).wait_recv()
    by_z[z] = by_y[...]
    for n in range(len(reach)):
        place_z(n).start()
    def halves_of(first, last, side, finish):
        def one(m, carry):
            for q in range(aux_count):
                lhs = jnp.concatenate([f_buf[q, m, s] for s in range(entries)], axis=1)
                blocks = c_far if side else c_near
                rhs = jnp.concatenate([blocks[cols[q, s, m]] for s in range(entries)], axis=1)
                done = lax.dot_general(lhs, rhs, NT, preferred_element_type=jnp.float32)
                at = q * all_occ + side * lanes
                half[m, :, at : at + lanes] = done.astype(jnp.bfloat16)
            if finish:
                mine[m] = half[m, pl.ds(pl.multiple_of(occ * rows, rows), rows), :]
            return carry

        lax.fori_loop(first, last, one, 0, unroll=6)

    for load in loads:
        load.wait()
    for n in (6, 11, 13):
        got(n)
    halves_of(0, nb // 4, 0, False)
    for n, nxt in ((7, 15), (8, 16), (9, 17), (10, 18)):
        got(n)
        go(nxt)
    for n in range(len(reach)):
        place_z(n, True).wait_recv()
    for n in range(len(reach), len(rounds)):
        place_z(n).start()
    halves_of(nb // 4, nb, 0, False)
    for n in (12, 14, 15, 16, 17, 18):
        got(n)
    halves_of(0, nb, 1, True)

    for n in range(len(reach), len(rounds)):
        place_z(n, True).wait_recv()
    fetch = pltpu.make_async_copy(by_z, place, p_in.at[0])
    fetch.start()

    def pair(p, carry):
        lhs = mine[...].reshape(nb * rows, aux_count * all_occ)
        rhs = half[pl.ds(2 * p, 2)].reshape(2 * blk, aux_count * all_occ)
        prod = lax.dot_general(lhs, rhs, NT, preferred_element_type=jnp.float32)
        tiles[pl.ds(2 * p * nb, nb)] = prod[:, :blk].reshape(nb, rows, blk)
        tiles[pl.ds((2 * p + 1) * nb, nb)] = prod[:, blk:].reshape(nb, rows, blk)
        return carry

    lax.fori_loop(0, nb // 2, pair, 0, unroll=6)

    fetch.wait()

    def post(n, part, axis_to):
        top = jnp.maximum(jnp.max(jnp.abs(part), axis=0, keepdims=True), 1e-30)
        count = part.shape[0]
        s_msg[n, :count] = jnp.round(part * (32767.0 / top)).astype(jnp.int32).astype(jnp.int16)
        s_scale[n] = top * (1.0 / 32767.0)
        sent.append((n, count, axis_to))
        for copy in copies(n, count, axis_to):
            copy.start()

    def copies(n, count, axis_to):
        piece = pl.ds(0, count)
        return (
            send(s_msg.at[n, piece], r_msg.at[n, piece], m_out.at[n], m_in.at[n], aux=axis_to),
            send(s_scale.at[n], r_scale.at[n], c_out.at[n], c_in.at[n], aux=axis_to),
        )

    def take(n, count):
        for copy in copies(n, count, y_to[0]):
            copy.wait_recv()
        return r_msg[n, :count].astype(jnp.int32).astype(jnp.float32) * r_scale[n]

    sent = []
    y_to = [up_y(1), up_y(NY - 1)]
    z_to = [up_z(1), up_z(NZ - 1)]
    far_to = [up_z(4), up_z(NZ - 4)]
    size, cut = own * rows, (own + 1) // 2 * rows
    halves = (cut, size - cut)
    msg_a, msg_b, msg_n, msg_q, msg_e, msg_m = 0, 16, 48, 64, 66, 68

    def chunk(up, d):
        yy, zz = (y + up) % NY, (z + d) % NZ
        return jnp.concatenate([tiles[place[zz, yy, 0, t]] for t in range(own)], axis=0)

    def near(up, d):
        return merged[up] if d == 0 else chunk(up, d)

    def way(d):
        return 0 if 1 <= d <= NZ // 2 else 1

    def first_hop(d):
        post(msg_a + d, near(2, d), y_to[way(d)])

    def second_hop(d):
        for w, up in ((0, 1), (1, NY - 1)):
            part = near(up, d)
            if way(d) == w:
                part = part + take(msg_a + d, size)
            post(msg_b + w * NZ + d, part, y_to[w])

    def column(d):
        part = near(0, d) + take(msg_b + d, size) + take(msg_b + NZ + d, size)
        if d % 4 == 0 and d != 8:
            kept[d // 4] = part
        elif d == 8:
            post(msg_q, part[:cut], far_to[0])
            post(msg_q + 1, part[cut:], far_to[1])
        else:
            hop = d % 4 if d < 8 else -(-d % 4)
            post(msg_n + d, part, up_z(hop % NZ))

    def merge_out():
        for up in (2, 1, 3, 0):
            for w, d in ((0, 1), (1, NZ - 1)):
                post(msg_m + w * NY + up, chunk(up, d), z_to[w])

    def merge_in():
        for up in (2, 1, 3, 0):
            merged[up] = chunk(up, 0) + take(msg_m + up, size) + take(msg_m + NY + up, size)

    def collect(d, others):
        part = kept[d // 4]
        for o in others:
            part = part + take(msg_n + o, size)
        return part

    def collect_mid(w):
        part = collect(*((4, (7, 6, 5)), (12, (9, 10, 11)))[w])
        came = take(msg_q + w, halves[w])
        if w == 0:
            part = jnp.concatenate([part[:cut] + came, part[cut:]], axis=0)
        else:
            part = jnp.concatenate([part[:cut], part[cut:] + came], axis=0)
        post(msg_e + w, part, far_to[w])

    count = len(ORDER)
    for i in range(-AHEAD, count + LAG):
        if i + AHEAD < count - 1:
            first_hop(ORDER[i + AHEAD])
        if i == MERGE_AT:
            merge_out()
        if i == count - 1 - LATE_BY:
            merge_in()
            first_hop(ORDER[-1])
        if 0 <= i < count:
            second_hop(ORDER[i])
        if i - LAG >= 0:
            column(ORDER[i - LAG])
        if i - LAG == MID_AT:
            collect_mid(0)
            collect_mid(1)
    part = collect(0, (3, 13, 2, 14))
    for w in range(2):
        part = part + take(msg_e + w, size)
    out[...] = part.reshape(own, rows, blk)

    for n, count, axis_to in sent:
        for copy in copies(n, count, axis_to):
            copy.wait_send()
    for n in range(len(moves)):
        pass_on(n).wait_send()
    for k in range(1, NY):
        place_y(k, y).wait_send()
    for n in range(len(rounds)):
        place_z(n).wait_send()


def shards(factor_tiles, tile_cols, coeffs, pair_owner):
    aux_count, nb, entries, blk, _ = factor_tiles.shape
    occ_ways = lax.axis_size("occ")
    rows = blk // occ_ways
    occ = coeffs.shape[1] * occ_ways
    own = pair_owner.shape[0]
    dma = pltpu.SemaphoreType.DMA
    vmem = pl.BlockSpec(memory_space=pltpu.VMEM)
    return pl.pallas_call(
        kernel,
        in_specs=[pl.BlockSpec(memory_space=pltpu.HBM)] * 4,
        out_specs=vmem,
        out_shape=jax.ShapeDtypeStruct((own, rows, blk), jnp.float32),
        scratch_shapes=[
            pltpu.SMEM((aux_count, entries, nb), jnp.int32),
            pltpu.SMEM((own,), jnp.int32),
            pltpu.VMEM(coeffs.shape[::-1], jnp.bfloat16),
            pltpu.VMEM(factor_tiles.shape, jnp.bfloat16),
            pltpu.VMEM((nb, occ // 2, blk), jnp.bfloat16),
            pltpu.VMEM((nb, occ // 2, blk), jnp.bfloat16),
            pltpu.VMEM((nb, blk, aux_count * occ), jnp.bfloat16),
            pltpu.VMEM((nb, rows, aux_count * occ), jnp.bfloat16),
            pltpu.VMEM((nb * nb, rows, blk), jnp.float32),
            pltpu.VMEM((NY, 1, 128), jnp.int32),
            pltpu.VMEM((NZ, NY, 1, 128), jnp.int32),
            pltpu.SMEM((NZ, NY, 1, 128), jnp.int32),
            pltpu.VMEM((MESSAGES, own * rows, blk), jnp.int16),
            pltpu.VMEM((MESSAGES, own * rows, blk), jnp.int16),
            pltpu.VMEM((MESSAGES, 1, blk), jnp.float32),
            pltpu.VMEM((MESSAGES, 1, blk), jnp.float32),
            pltpu.VMEM((4, own * rows, blk), jnp.float32),
            pltpu.VMEM((NY, own * rows, blk), jnp.float32),
            dma((3,)),
            dma((STAGES,)),
            dma((19,)), dma((19,)),
            dma((NY - 1,)), dma((NY - 1,)),
            dma((NZ - 1,)), dma((NZ - 1,)),
            dma((1,)),
            dma((MESSAGES,)), dma((MESSAGES,)),
            dma((MESSAGES,)), dma((MESSAGES,)),
        ],
        compiler_params=pltpu.CompilerParams(
            collective_id=0, has_side_effects=True, vmem_limit_bytes=61 * 2**20
        ),
    )(jnp.transpose(tile_cols, (0, 2, 1)), pair_owner, factor_tiles, coeffs.T)


def solution(mesh):
    placed = (P("aux", None, None, None, None), P("aux", None, None), P(None, "occ"), P("aux"))
    return jax.shard_map(
        shards, mesh=mesh, in_specs=placed, out_specs=P("aux", "occ", None), check_vma=False
    )
```
